32 devices in a mesh: grp: 2 (over x), blk: 16 (over z, y, core).
Axes of the slice: x: 2, y: 2, z: 4, core: 2. Of those that a mesh axis runs over, the one named last changes fastest.
Arguments:
- feats: bfloat16 [65536, 128], P(('grp', 'blk')), parts along dimension 0, may hold values from -6 to 6
- node_order: int32 [65536], P(('grp', 'blk')), parts along dimension 0, may hold values from 0 to 32767, as said below
- weight: bfloat16 [128, 128], replicated, may hold values from -0.5 to 0.5
- bias: float32 [128], replicated, may hold values from -3 to 3
- block_vals: bfloat16 [10752, 128, 128], P(('grp', 'blk')), parts along dimension 0, may hold values from -0.15625 to 0.15625
- block_rows: int32 [10752], P(('grp', 'blk')), parts along dimension 0, may hold values from 0 to 255, as said below
- block_cols: int32 [10752], P(('grp', 'blk')), parts along dimension 0, may hold values from 0 to 255, as said below
- block_counts: int32 [32], P(('grp', 'blk')), parts along dimension 0, may hold values from 112 to 336, as said below
- cotangent: bfloat16 [65536, 128], P(('grp', 'blk')), parts along dimension 0, may hold values from -6 to 6
Outputs:
- activation: bfloat16 [65536, 128], P(('grp', 'blk')), parts along dimension 0
- grad_feats: bfloat16 [65536, 128], P(('grp', 'blk')), parts along dimension 0
- grad_weight: float32 [256, 128], P('grp'), parts along dimension 0
- grad_bias: float32 [256], P('grp'), parts along dimension 0
The draws below stay inside these ranges and needn't reach their ends.
There are 2 independent parts, one for each index of `grp`. The reference program is written for one: setup_inputs(seed, part) draws one part's arguments, and reference() takes and returns one part's arrays. A program takes and returns all parts, laid end to end along the dimension named above; an argument that names none is the same for every part. Nothing has to cross between parts.
Inputs may be any that keep to these rules, and one draw needn't show every extreme that they name: On every device some permutation maps its own 2048 rows onto themselves: node_order of a device's rows names stored rows of that same device. `block_rows`: slot s of the whole array lies on device s // 336 and names one of that device's own 16 row panels. `block_cols`: slot s names a column panel of a device at most 4 steps from device s // 336 around the closed loop of devices (indices taken modulo the device count). `block_counts`: in every draw some device has exactly 336 live slots.
All inputs are finite; a program needn't handle non-finite values.
Results may differ from the reference program's by a relative error of at most 0.0061.
Values may be sent and summed in bfloat16 or wider, within the bound.
A program may use at most 128 MiB of HBM per device.

```python
import jax
import jax.numpy as jnp
from jax import lax

F = 128
H = 128
BS = 128
REACH = 4
PANELS_DEV = 16
CAP = 336
ROWS_DEV = 2048
NODES = 32768
PANELS = 256
BLOCKS = 5376
N_BLK = 16


def draw_node_order(key, part):
    key = jax.random.fold_in(key, 11)
    keys = jax.random.split(key, N_BLK)
    perms = jax.vmap(lambda k: jax.random.permutation(k, ROWS_DEV))(keys)
    base = (jnp.arange(N_BLK, dtype=jnp.int32) * ROWS_DEV)[:, None]
    return (perms.astype(jnp.int32) + base).reshape(NODES)


def draw_block_rows(key, part):
    key = jax.random.fold_in(key, 12)
    device = jnp.arange(BLOCKS, dtype=jnp.int32) // CAP
    local = jax.random.randint(key, (BLOCKS,), 0, PANELS_DEV, dtype=jnp.int32)
    return device * PANELS_DEV + local


def draw_block_cols(key, part):
    key = jax.random.fold_in(key, 13)
    key_off, key_pan = jax.random.split(key)
    device = jnp.arange(BLOCKS, dtype=jnp.int32) // CAP
    offset = jax.random.randint(key_off, (BLOCKS,), -REACH, REACH + 1, dtype=jnp.int32)
    target = jnp.mod(device + offset + N_BLK, N_BLK)
    local = jax.random.randint(key_pan, (BLOCKS,), 0, PANELS_DEV, dtype=jnp.int32)
    return target * PANELS_DEV + local


def draw_block_counts(key, part):
    key = jax.random.fold_in(key, 14)
    key_cnt, key_top = jax.random.split(key)
    counts = jax.random.randint(key_cnt, (N_BLK,), CAP // 3, 2 * CAP // 3 + 1, dtype=jnp.int32)
    fullest = jax.random.randint(key_top, (), 0, N_BLK, dtype=jnp.int32)
    return jnp.where(jnp.arange(N_BLK, dtype=jnp.int32) == fullest, jnp.int32(CAP), counts)


def steps_of(stream_key, dims, cuts, smallest, high):
    gain, own = 1.0, jax.random.fold_in(stream_key, 6)
    for position, blocks in cuts:
        draws = jnp.exp(jax.random.uniform(jax.random.fold_in(own, position), (blocks,), jnp.float32, smallest / len(cuts), high / len(cuts)))
        gain = gain * jnp.repeat(draws, dims[position] // blocks).reshape([-1 if axis == position else 1 for axis in range(len(dims))])
    return gain


def scatter_about(stream_key, shape, scale, limit, pieces=(), held_as=jnp.bfloat16):
    gain = steps_of(stream_key, shape, pieces, -0.22, 0.18) if pieces else 1.0
    result = jax.random.normal(stream_key, shape, jnp.float32) * scale * gain
    return jnp.minimum(jnp.maximum(result, -limit), limit).astype(held_as)


def setup_inputs(seed: int = 0, part: int = 0) -> dict:
    arg_keys = jax.random.split(jax.random.key(seed), 10)
    part_splits = jax.random.split(jax.random.fold_in(arg_keys[9], part), 10)
    return {
        "feats": scatter_about(part_splits[0], (NODES, F), 1.0, 6.0, ((0, 16),)),
        "node_order": draw_node_order(jax.random.fold_in(jax.random.fold_in(arg_keys[9], part), 71), part),
        "weight": scatter_about(arg_keys[2], (F, H), F ** -0.5, 0.5),
        "bias": scatter_about(arg_keys[3], (H,), 0.5, 3.0, (), jnp.float32),
        "block_vals": scatter_about(part_splits[4], (BLOCKS, BS, BS), (BS * CAP // (2 * PANELS_DEV)) ** -0.5, 0.15625, ((0, 16),)),
        "block_rows": draw_block_rows(jax.random.fold_in(jax.random.fold_in(arg_keys[9], part), 71), part),
        "block_cols": draw_block_cols(jax.random.fold_in(jax.random.fold_in(arg_keys[9], part), 71), part),
        "block_counts": draw_block_counts(jax.random.fold_in(jax.random.fold_in(arg_keys[9], part), 71), part),
        "cotangent": scatter_about(part_splits[8], (NODES, H), 1.0, 6.0, ((0, 16),)),
    }


def reference(feats, node_order, weight, bias, block_vals, block_rows, block_cols, block_counts, cotangent):
    nodes = feats[node_order]
    projected = jnp.dot(nodes, weight, preferred_element_type=jnp.float32).astype(jnp.bfloat16)
    panel_all = projected.reshape(PANELS, BS, H).astype(jnp.float32)
    vals = block_vals.reshape(N_BLK, CAP, BS, BS)
    rows = block_rows.reshape(N_BLK, CAP)
    cols = block_cols.reshape(N_BLK, CAP)
    slot_ids = jnp.arange(CAP, dtype=jnp.int32)
    live = slot_ids[None, :] < block_counts[:, None]
    device_ids = jnp.arange(N_BLK, dtype=jnp.int32)
    panel_ids = jnp.arange(PANELS_DEV, dtype=jnp.int32)

    def forward(items):
        vblk, rblk, cblk, lblk, device = items
        masked = jnp.where(lblk[:, None, None], vblk.astype(jnp.float32), jnp.float32(0.0))
        inputs = panel_all[cblk]
        prod = jnp.einsum('bij,bjh->bih', masked, inputs, precision=lax.Precision.HIGHEST)
        onehot = ((rblk - device * PANELS_DEV)[None, :] == panel_ids[:, None]).astype(jnp.float32)
        return jnp.einsum('pb,bih->pih', onehot, prod, precision=lax.Precision.HIGHEST)

    summed = lax.map(forward, (vals, rows, cols, live, device_ids)).reshape(NODES, H)
    mixed = summed + bias
    sig = jax.nn.sigmoid(mixed)
    activation = (mixed * sig).astype(jnp.bfloat16)
    grad_mixed = (cotangent.astype(jnp.float32) * sig * (1.0 + mixed * (1.0 - sig))).astype(jnp.bfloat16)
    grad_bias = jnp.sum(grad_mixed.astype(jnp.float32), axis=0)
    grad_panels = grad_mixed.reshape(PANELS, BS, H).astype(jnp.float32)

    def backward(acc, items):
        vblk, rblk, cblk, lblk = items
        masked = jnp.where(lblk[:, None, None], vblk.astype(jnp.float32), jnp.float32(0.0))
        contrib = jnp.einsum('bji,bjh->bih', masked, grad_panels[rblk], precision=lax.Precision.HIGHEST)
        return acc.at[cblk].add(contrib), None

    start = jnp.zeros((PANELS, BS, H), jnp.float32)
    grad_proj, unused = lax.scan(backward, start, (vals, rows, cols, live))
    grad_low = grad_proj.reshape(NODES, H).astype(jnp.bfloat16)
    grad_weight = jnp.dot(nodes.T, grad_low, preferred_element_type=jnp.float32)
    grad_feats = jnp.dot(grad_low, weight.T, preferred_element_type=jnp.float32).astype(jnp.bfloat16)
    return activation, grad_feats, grad_weight, grad_bias
```

```python
import functools

import jax
import jax.numpy as jnp
from jax import lax
from jax.experimental import pallas as pl
from jax.experimental.pallas import tpu as pltpu
from jax.sharding import PartitionSpec as P

QUAD = 4
CHUNKS = 12
UNROLL = 4
BF = jnp.bfloat16
F32 = jnp.float32
MESH = pl.DeviceIdType.MESH
VMEM_LIMIT = 58 * 1024 * 1024


def vmem():
    return pl.BlockSpec(memory_space=pltpu.VMEM)


def smem():
    return pl.BlockSpec(memory_space=pltpu.SMEM)


def gather_kernel(order, feats, weight, nodes, projected, wide, picked):
    count = feats.shape[0]
    wide[...] = feats[...].astype(F32)

    def body(i, carry):
        base = pl.multiple_of(i * 16, 16)
        for u in range(16):
            src = lax.rem(order[base + u], count)
            picked[pl.ds(base + u, 1), :] = wide[pl.ds(src, 1), :]
        return carry

    lax.fori_loop(0, count // 16, body, 0)
    part = 512 if count % 512 == 0 else count

    def product(i, carry):
        at = pl.ds(pl.multiple_of(i * part, part), part)
        rows = picked[at, :].astype(BF)
        nodes[at, :] = rows
        projected[at, :] = jnp.dot(rows, weight[...], preferred_element_type=F32).astype(BF)
        return carry

    lax.fori_loop(0, count // part, product, 0)


def places(n):
    me = lax.axis_index("blk")
    q, j = me // QUAD, me % QUAD
    y, c = j // 2, j % 2
    quads = n // QUAD
    up = ((q + 1) % quads) * QUAD + j
    down = ((q + quads - 1) % quads) * QUAD + j
    across = q * QUAD + (1 - y) * 2 + c
    twin = q * QUAD + y * 2 + (1 - c)
    return me, q, j, y, c, up, down, across, twin


def greet(devices):
    barrier = pltpu.get_barrier_semaphore()
    for device in devices:
        pl.semaphore_signal(
            barrier, inc=1, device_id=(lax.axis_index("grp"), device), device_id_type=MESH
        )
    pl.semaphore_wait(barrier, len(devices))


def send(src, dst, send_sem, recv_sem, device):
    copy = pltpu.make_async_remote_copy(
        src_ref=src,
        dst_ref=dst,
        send_sem=send_sem,
        recv_sem=recv_sem,
        device_id=(lax.axis_index("grp"), device),
        device_id_type=MESH,
    )
    copy.start()
    return copy


def window_kernel(n, own, window, send_sem, recv_sem, local_sem):
    me, q, j, y, c, up, down, across, twin = places(n)
    nj = (1 - y) * 2 + c
    tj = y * 2 + (1 - c)
    fj = (1 - y) * 2 + (1 - c)
    beyond = (1 - y) * up + y * down
    half = own.shape[0] // 2
    greet((up, down, across, twin))
    sent = []

    def piece(slot, p, h):
        return window.at[slot * QUAD + p, pl.ds(h * half, half), :]

    def push(src, slot, p, h, device):
        k = len(sent)
        sent.append(
            send(src, piece(slot, p, h), send_sem.at[k], recv_sem.at[slot * QUAD + p, h], device)
        )

    def arrived(slot, p, h):
        spot = piece(slot, p, h)
        pltpu.make_async_remote_copy(
            src_ref=spot,
            dst_ref=spot,
            send_sem=send_sem.at[0],
            recv_sem=recv_sem.at[slot * QUAD + p, h],
            device_id=(lax.axis_index("grp"), twin),
            device_id_type=MESH,
        ).wait_recv()
        return spot

    for h in (1, 0):
        mine = own.at[pl.ds(h * half, half), :]
        push(mine, 1, j, h, across)
        push(mine, 0, j, h, up)
        push(mine, 2, j, h, down)
        push(mine, 1, j, h, twin)
    keep = pltpu.make_async_copy(own, window.at[QUAD + j], local_sem)
    keep.start()

    spot = arrived(1, nj, 1)
    push(spot, 2 * y, nj, 1, beyond)
    push(spot, 1, nj, 1, twin)
    near, other = 2 * (1 - y), 2 * y
    zs = 2 * (1 - c)
    zo = 2 * c
    for h in (1, 0):
        if h == 0:
            spot = arrived(1, nj, 0)
            push(spot, 1, nj, 0, twin)
        spot = arrived(near, j, h)
        if h == 0:
            push(spot, near, j, 0, across)
        arrived(other, j, h)
        push(piece(zs, j, h), zs, j, h, twin)
    for h in (1, 0):
        spot = arrived(2 * y, nj, h)
        push(spot, 2 * y, nj, h, twin)
    for h in (1, 0):
        arrived(1, tj, h)
        arrived(1, fj, h)
        arrived(zo, tj, h)
        arrived(2 * y, fj, h)
    keep.wait()
    for copy in sent:
        copy.wait_send()


def spmm_kernel(
    counts, rows, cols, window, bias, cotangent, vals_hbm,
    act, partial, grad_bias, vals, acc, flipped, grads, sems,
):
    slots, side, width = vals_hbm.shape
    panels = acc.shape[0] - 1
    spread = grads.shape[0] - 1
    per = slots // CHUNKS
    count = counts[0]

    def fetch(k):
        at = pl.ds(k * per, per)
        return pltpu.make_async_copy(vals_hbm.at[at], vals.at[at], sems.at[k])

    for k in range(CHUNKS):
        @pl.when(k * per < count)
        def _(k=k):
            fetch(k).start()

    acc[...] = jnp.zeros_like(acc)

    def forward(i, carry):
        at = [i * UNROLL + u for u in range(UNROLL)]
        prods = [
            jnp.dot(vals[s], window[cols[s]], preferred_element_type=F32) for s in at
        ]
        for s, prod in zip(at, prods):
            row = jnp.where(s < count, rows[s], panels)
            acc[row] += prod
        return carry

    for k in range(CHUNKS):
        @pl.when(k * per < count)
        def _(k=k):
            fetch(k).wait()
            lax.fori_loop(k * per // UNROLL, (k + 1) * per // UNROLL, forward, 0)

    def clear(p, carry):
        grads[p] = jnp.zeros((side, width), F32)
        return carry

    lax.fori_loop(0, spread, clear, 0)

    def middle(r, total):
        mixed = acc[r] + bias[...]
        sig = 1.0 / (1.0 + jnp.exp(-mixed))
        act[r] = (mixed * sig).astype(BF)
        grad = cotangent[r].astype(F32) * sig * (1.0 + mixed * (1.0 - sig))
        low = grad.astype(BF).astype(F32)
        flipped[r] = low.T.astype(BF)
        return total + jnp.sum(low.reshape(side // 8, 8, width), axis=0)

    grad_bias[...] = lax.fori_loop(0, panels, middle, jnp.zeros((8, width), F32))

    def backward(i, carry):
        at = [i * UNROLL + u for u in range(UNROLL)]
        prods = [
            jnp.dot(flipped[rows[s]], vals[s], preferred_element_type=F32) for s in at
        ]
        for s, prod in zip(at, prods):
            col = jnp.where(s < count, cols[s], spread)
            grads[col] += prod
        return carry

    lax.fori_loop(0, (count + UNROLL - 1) // UNROLL, backward, 0)

    def store(p, carry):
        partial[p] = grads[p].astype(BF)
        return carry

    lax.fori_loop(0, spread, store, 0)


def reduce_kernel(
    n, shared, partial, nodes, weight, grad_bias,
    grad_feats, grad_weight, bias_out,
    from_twin, from_across, from_z, far_across, far_z, mid, work,
    share, gathered, biases, own_bias,
    send_sem, recv_sem, small_send, small_recv,
):
    me, q, j, y, c, up, down, across, twin = places(n)
    nj = (1 - y) * 2 + c
    tj = y * 2 + (1 - c)
    fj = (1 - y) * 2 + (1 - c)
    panels = partial.shape[1]
    half = panels // 2
    if shared:
        greet([(me + d) % n for d in range(1, n)])
    else:
        greet((up, down, across, twin))
    sent = []

    def push(src, dst, key, device):
        k = len(sent)
        copy = send(src, dst, send_sem.at[k], recv_sem.at[key], device)
        sent.append(copy)

    def arrived(dst, key):
        pltpu.make_async_remote_copy(
            src_ref=dst,
            dst_ref=dst,
            send_sem=send_sem.at[0],
            recv_sem=recv_sem.at[key],
            device_id=(lax.axis_index("grp"), twin),
            device_id_type=MESH,
        ).wait_recv()

    def part(ref, index, h):
        return ref.at[index, pl.ds(h * half, half)]

    def merge(dst, a, b):
        def body(p, carry):
            dst[p] = (a[p].astype(F32) + b[p].astype(F32)).astype(BF)
            return carry

        lax.fori_loop(0, half, body, 0)

    order = [
        (0, 2 * y * QUAD + fj),
        (1, QUAD + fj),
        (2, 2 * c * QUAD + tj),
        (3, QUAD + tj),
    ]
    for k, index in order:
        for h in (1, 0):
            push(part(partial, index, h), part(from_twin, k, h), 2 * k + h, twin)
    if shared:
        small = []
        own_bias[...] = grad_bias[...]
        for d in range(1, n):
            small.append(
                send(own_bias, biases.at[me], small_send.at[0, d], small_recv.at[0, me],
                     (me + d) % n)
            )
        biases[me] = grad_bias[...]

    back = (1 - y) * down + y * up
    for h in (1, 0):
        arrived(part(from_twin, 0, h), h)
        merge(part(mid, 0, h), part(partial, 2 * y * QUAD + nj, h), part(from_twin, 0, h))
        if h == 1:
            push(part(mid, 0, 1), far_z, 8, back)
        else:
            push(part(mid, 0, 0), far_across, 9, across)
    near, other = 2 * (1 - y), 2 * y
    zs, zo = 2 * (1 - c), 2 * c
    for h in (1, 0):
        arrived(part(from_twin, 2, h), 4 + h)
        merge(part(mid, 2, h), part(partial, zs * QUAD + j, h), part(from_twin, 2, h))

        def fill(p, carry, h=h):
            mid[1, h * half + p] = partial[zo * QUAD + j, h * half + p]
            return carry

        lax.fori_loop(0, half, fill, 0)
    near_at = 1 + (near == zs).astype(jnp.int32)
    zs_up = (zs == 2).astype(jnp.int32)
    to_zs = zs_up * up + (1 - zs_up) * down
    to_zo = (1 - zs_up) * up + zs_up * down
    push(part(mid, 2, 1), part(from_z, 1 - zs_up, 1), 10 + 2 * (1 - zs_up) + 1, to_zs)
    push(part(mid, 1, 1), part(from_z, zs_up, 1), 10 + 2 * zs_up + 1, to_zo)
    arrived(far_across, 9)
    merge(part(mid, near_at, 0), part(mid, near_at, 0), far_across)
    push(part(mid, 2, 0), part(from_z, 1 - zs_up, 0), 10 + 2 * (1 - zs_up), to_zs)
    push(part(mid, 1, 0), part(from_z, zs_up, 0), 10 + 2 * zs_up, to_zo)
    arrived(part(from_twin, 1, 0), 2)
    merge(part(mid, 3, 0), part(partial, QUAD + nj, 0), part(from_twin, 1, 0))
    push(part(mid, 3, 0), part(from_across, 0, 0), 14, across)
    arrived(part(from_twin, 1, 1), 3)
    merge(part(mid, 3, 1), part(partial, QUAD + nj, 1), part(from_twin, 1, 1))
    arrived(far_z, 8)
    merge(part(mid, 3, 1), part(mid, 3, 1), far_z)
    push(part(mid, 3, 1), part(from_across, 0, 1), 15, across)

    work[...] = jnp.zeros_like(work)
    for h in (0, 1):
        arrived(part(from_twin, 3, h), 6 + h)
        arrived(part(from_z, 0, h), 10 + h)
        arrived(part(from_z, 1, h), 12 + h)
        arrived(part(from_across, 0, h), 14 + h)

        def finish(i, carry, h=h):
            p = h * half + i
            total = partial[QUAD + j, p].astype(F32) + from_twin[3, p].astype(F32)
            total = total + from_across[0, p].astype(F32)
            total = total + from_z[0, p].astype(F32) + from_z[1, p].astype(F32)
            low = total.astype(BF)
            work[...] += jnp.dot(low, nodes[p], preferred_element_type=F32)
            flat = total.T.astype(BF)
            grad_feats[p] = lax.dot_general(
                flat, weight[...], (((1,), (1,)), ((), ())), preferred_element_type=F32
            ).astype(BF)
            return carry

        lax.fori_loop(0, half, finish, 0)

    if shared:
        step = work.shape[0] // n

        def small_wait(dst, level, source):
            pltpu.make_async_remote_copy(
                src_ref=dst,
                dst_ref=dst,
                send_sem=small_send.at[0, 0],
                recv_sem=small_recv.at[level, source],
                device_id=(lax.axis_index("grp"), twin),
                device_id_type=MESH,
            ).wait_recv()

        for d in range(1, n):
            peer = (me + d) % n
            small.append(
                send(work.at[pl.ds(peer * step, step), :], share.at[me],
                     small_send.at[1, d], small_recv.at[1, me], peer)
            )
        share[me] = work[pl.ds(pl.multiple_of(me * step, step), step), :]
        for d in range(1, n):
            small_wait(share.at[(me + d) % n], 1, (me + d) % n)
        gathered[me] = jnp.sum(share[...], axis=0)
        for d in range(1, n):
            small.append(
                send(gathered.at[me], gathered.at[me], small_send.at[2, d],
                     small_recv.at[2, me], (me + d) % n)
            )
        for d in range(1, n):
            small_wait(biases.at[(me + d) % n], 0, (me + d) % n)
        bias_out[...] = jnp.sum(jnp.sum(biases[...], axis=0), axis=0, keepdims=True)
        for d in range(1, n):
            small_wait(gathered.at[(me + d) % n], 2, (me + d) % n)
        grad_weight[...] = gathered[...].reshape(work.shape).T
        for copy in small:
            copy.wait_send()
    else:
        grad_weight[...] = work[...].T
        bias_out[...] = jnp.sum(grad_bias[...], axis=0, keepdims=True)
    for copy in sent:
        copy.wait_send()


def on_device(
    feats, node_order, weight, bias, block_vals, block_rows, block_cols, block_counts, cotangent
):
    row_count, width_in = feats.shape
    slots, side, _ = block_vals.shape
    width = weight.shape[1]
    panels = row_count // side
    n = lax.axis_size("blk")
    quads = n // QUAD
    pieces = 3 * QUAD
    me = lax.axis_index("blk")

    rows = block_rows - me * panels
    owner = block_cols // panels
    slot = jnp.mod(owner // QUAD - me // QUAD + 1 + quads, quads)
    cols = (slot * QUAD + owner % QUAD) * panels + block_cols % panels

    nodes, projected = pl.pallas_call(
        gather_kernel,
        out_shape=(
            jax.ShapeDtypeStruct((row_count, width_in), BF),
            jax.ShapeDtypeStruct((row_count, width), BF),
        ),
        in_specs=[smem(), vmem(), vmem()],
        out_specs=(vmem(), vmem()),
        scratch_shapes=[
            pltpu.VMEM((row_count, width_in), F32),
            pltpu.VMEM((row_count, width_in), F32),
        ],
        compiler_params=pltpu.CompilerParams(vmem_limit_bytes=VMEM_LIMIT),
        name="gather_project",
    )(node_order, feats, weight)

    window = pl.pallas_call(
        functools.partial(window_kernel, n),
        out_shape=jax.ShapeDtypeStruct((pieces, row_count, width), BF),
        in_specs=[vmem()],
        out_specs=vmem(),
        scratch_shapes=[
            pltpu.SemaphoreType.DMA((24,)),
            pltpu.SemaphoreType.DMA((pieces, 2)),
            pltpu.SemaphoreType.DMA,
        ],
        compiler_params=pltpu.CompilerParams(
            collective_id=0, has_side_effects=True, vmem_limit_bytes=VMEM_LIMIT
        ),
        name="window",
    )(projected)

    spread = pieces * panels
    act, partial, bias_part = pl.pallas_call(
        spmm_kernel,
        out_shape=(
            jax.ShapeDtypeStruct((panels, side, width), BF),
            jax.ShapeDtypeStruct((spread, width, side), BF),
            jax.ShapeDtypeStruct((8, width), F32),
        ),
        in_specs=[smem(), smem(), smem(), vmem(), vmem(), vmem(), pl.BlockSpec(memory_space=pl.ANY)],
        out_specs=(vmem(), vmem(), vmem()),
        scratch_shapes=[
            pltpu.VMEM((slots, side, side), BF),
            pltpu.VMEM((panels + 1, side, width), F32),
            pltpu.VMEM((panels, width, side), BF),
            pltpu.VMEM((spread + 1, width, side), F32),
            pltpu.SemaphoreType.DMA((CHUNKS,)),
        ],
        compiler_params=pltpu.CompilerParams(vmem_limit_bytes=VMEM_LIMIT),
        name="sparse_products",
    )(
        block_counts, rows, cols,
        window.reshape(spread, side, width), bias.reshape(1, width),
        cotangent.reshape(panels, side, width), block_vals,
    )

    shared = width % (8 * n) == 0
    few = n if shared else 1
    step = width // n if shared else 8
    grad_feats, grad_weight, grad_bias = pl.pallas_call(
        functools.partial(reduce_kernel, n, shared),
        out_shape=(
            jax.ShapeDtypeStruct((panels, side, width_in), BF),
            jax.ShapeDtypeStruct((width_in, width), F32),
            jax.ShapeDtypeStruct((1, width), F32),
        ),
        in_specs=[vmem()] * 4,
        out_specs=(vmem(), vmem(), vmem()),
        scratch_shapes=[
            pltpu.VMEM((4, panels, width, side), BF),
            pltpu.VMEM((1, panels, width, side), BF),
            pltpu.VMEM((2, panels, width, side), BF),
            pltpu.VMEM((panels // 2, width, side), BF),
            pltpu.VMEM((panels // 2, width, side), BF),
            pltpu.VMEM((4, panels, width, side), BF),
            pltpu.VMEM((width, width_in), F32),
            pltpu.VMEM((few, step, width_in), F32),
            pltpu.VMEM((few, step, width_in), F32),
            pltpu.VMEM((few, 8, width), F32),
            pltpu.VMEM((8, width), F32),
            pltpu.SemaphoreType.DMA((16,)),
            pltpu.SemaphoreType.DMA((16,)),
            pltpu.SemaphoreType.DMA((3, few)),
            pltpu.SemaphoreType.DMA((3, few)),
        ],
        compiler_params=pltpu.CompilerParams(
            collective_id=1, has_side_effects=True, vmem_limit_bytes=VMEM_LIMIT
        ),
        name="reduce_back",
    )(
        partial.reshape(pieces, panels, width, side),
        nodes.reshape(panels, side, width_in), weight, bias_part,
    )
    grad_bias = grad_bias.reshape(width)
    if not shared:
        grad_weight, grad_bias = lax.psum((grad_weight, grad_bias), "blk")
    return (
        act.reshape(row_count, width),
        grad_feats.reshape(row_count, width_in),
        grad_weight,
        grad_bias,
    )


def solution(mesh):
    in_specs = (
        P(("grp", "blk"), None),
        P(("grp", "blk")),
        P(),
        P(),
        P(("grp", "blk"), None, None),
        P(("grp", "blk")),
        P(("grp", "blk")),
        P(("grp", "blk")),
        P(("grp", "blk"), None),
    )
    out_specs = (P(("grp", "blk"), None), P(("grp", "blk"), None), P("grp", None), P("grp"))
    return jax.shard_map(
        on_device, mesh=mesh, in_specs=in_specs, out_specs=out_specs, check_vma=False
    )
```

```python
import functools

import jax
import jax.numpy as jnp
from jax import lax
from jax.experimental import pallas as pl
from jax.experimental.pallas import tpu as pltpu
from jax.sharding import PartitionSpec as P

QUAD = 4
CHUNKS = 7
UNROLL = 16
PARTS = 8
RELAYED = 0
BF = jnp.bfloat16
F32 = jnp.float32
MESH = pl.DeviceIdType.MESH
VMEM_LIMIT = 58 * 1024 * 1024


def vmem():
    return pl.BlockSpec(memory_space=pltpu.VMEM)


def anywhere():
    return pl.BlockSpec(memory_space=pl.ANY)


def smem():
    return pl.BlockSpec(memory_space=pltpu.SMEM)


def gather_kernel(order, feats, weight, nodes, projected, wide, picked):
    count = feats.shape[0]
    first = lax.axis_index("blk") * count
    wide[...] = feats[...].astype(F32)

    def body(i, carry):
        base = pl.multiple_of(i * 16, 16)
        taken = [wide[pl.ds(order[base + u] - first, 1), :] for u in range(16)]
        for u in range(16):
            picked[pl.ds(base + u, 1), :] = taken[u]
        return carry

    lax.fori_loop(0, count // 16, body, 0)
    part = 512 if count % 512 == 0 else count

    def product(i, carry):
        at = pl.ds(pl.multiple_of(i * part, part), part)
        rows = picked[at, :].astype(BF)
        nodes[at, :] = rows
        projected[at, :] = jnp.dot(rows, weight[...], preferred_element_type=F32).astype(BF)
        return carry

    lax.fori_loop(0, count // part, product, 0)


def places(n):
    me = lax.axis_index("blk")
    q, j = me // QUAD, me % QUAD
    y, c = j // 2, j % 2
    quads = n // QUAD
    up = ((q + 1) % quads) * QUAD + j
    down = ((q + quads - 1) % quads) * QUAD + j
    across = q * QUAD + (1 - y) * 2 + c
    twin = q * QUAD + y * 2 + (1 - c)
    return me, q, j, y, c, up, down, across, twin


def greet(devices):
    barrier = pltpu.get_barrier_semaphore()
    for device in devices:
        pl.semaphore_signal(
            barrier, inc=1, device_id=(lax.axis_index("grp"), device), device_id_type=MESH
        )
    pl.semaphore_wait(barrier, len(devices))


def send(src, dst, send_sem, recv_sem, device):
    copy = pltpu.make_async_remote_copy(
        src_ref=src,
        dst_ref=dst,
        send_sem=send_sem,
        recv_sem=recv_sem,
        device_id=(lax.axis_index("grp"), device),
        device_id_type=MESH,
    )
    copy.start()
    return copy


def window_kernel(n, own, window, send_sem, recv_sem, local_sem):
    me, q, j, y, c, up, down, across, twin = places(n)
    nj = (1 - y) * 2 + c
    tj = y * 2 + (1 - c)
    fj = (1 - y) * 2 + (1 - c)
    beyond = (1 - y) * up + y * down
    half = own.shape[0] // PARTS
    greet((up, down, across, twin))
    sent = []

    def piece(slot, p, h):
        return window.at[slot * QUAD + p, pl.ds(h * half, half), :]

    def push(src, slot, p, h, device):
        k = len(sent)
        sent.append(
            send(src, piece(slot, p, h), send_sem.at[k], recv_sem.at[slot * QUAD + p, h], device)
        )

    def arrived(slot, p, h):
        spot = piece(slot, p, h)
        pltpu.make_async_remote_copy(
            src_ref=spot,
            dst_ref=spot,
            send_sem=send_sem.at[0],
            recv_sem=recv_sem.at[slot * QUAD + p, h],
            device_id=(lax.axis_index("grp"), twin),
            device_id_type=MESH,
        ).wait_recv()
        return spot

    def mine(h):
        return own.at[pl.ds(h * half, half), :]

    direct = PARTS - RELAYED
    near, other = 2 * (1 - y), 2 * y
    zs, zo = 2 * (1 - c), 2 * c
    for i in range(PARTS):
        push(mine(PARTS - 1 - i), 1, j, PARTS - 1 - i, across)
        push(mine(i), 0, j, i, up)
        push(mine(i), 2, j, i, down)
    for h in range(PARTS):
        push(mine(h), 1, j, h, twin)
    keep = pltpu.make_async_copy(own, window.at[QUAD + j], local_sem)
    keep.start()
    for i in range(PARTS):
        h = PARTS - 1 - i
        spot = arrived(1, nj, h)
        if h >= direct:
            push(spot, 2 * y, nj, h, beyond)
        push(spot, 1, nj, h, twin)
        spot = arrived(near, j, i)
        if i < direct:
            push(spot, near, j, i, across)
        arrived(other, j, i)
        push(piece(zs, j, i), zs, j, i, twin)
    far = []
    for i in range(PARTS):
        far += [h for h in (PARTS - 1 - i, i) if h not in far]
    for h in far:
        push(arrived(2 * y, nj, h), 2 * y, nj, h, twin)
    for h in range(PARTS):
        arrived(1, tj, h)
        arrived(1, fj, h)
        arrived(zo, tj, h)
        arrived(2 * y, fj, h)
    keep.wait()
    for copy in sent:
        copy.wait_send()


def spmm_kernel(
    n, counts, block_rows, block_cols, window_hbm, bias, cotangent, vals_hbm,
    act, partial, grad_bias, vals, window, acc, flipped, grads, sems, window_sem,
):
    slots, side, width = vals_hbm.shape
    panels = acc.shape[0] - 1
    spread = grads.shape[0] - 1
    per = slots // CHUNKS
    count = counts[0]
    me = lax.axis_index("blk")
    quads = n // QUAD
    first_row = me * panels
    first_col = lax.rem(me // QUAD + quads - 1, quads) * (QUAD * panels)
    fill = pltpu.make_async_copy(window_hbm, window, window_sem)
    fill.start()

    def row_of(s):
        return block_rows[s] - first_row

    def col_of(s):
        away = block_cols[s] - first_col
        return jnp.where(away < 0, away + n * panels, away)

    def fetch(k):
        at = pl.ds(k * per, per)
        return pltpu.make_async_copy(vals_hbm.at[at], vals.at[at], sems.at[k])

    for k in range(CHUNKS):
        @pl.when(k * per < count)
        def _(k=k):
            fetch(k).start()

    acc[...] = jnp.zeros_like(acc)

    def clear(p, carry):
        grads[p] = jnp.zeros((side, width), F32)
        return carry

    lax.fori_loop(0, spread, clear, 0)
    fill.wait()

    def forward(i, carry):
        at = [i * UNROLL + u for u in range(UNROLL)]
        prods = [
            jnp.dot(vals[s], window[col_of(s)], preferred_element_type=F32) for s in at
        ]
        for s, prod in zip(at, prods):
            row = jnp.where(s < count, row_of(s), panels)
            acc[row] += prod
        return carry

    for k in range(CHUNKS):
        @pl.when(k * per < count)
        def _(k=k):
            fetch(k).wait()
            lax.fori_loop(k * per // UNROLL, (k + 1) * per // UNROLL, forward, 0)

    def middle(r, total):
        mixed = acc[r] + bias[...]
        sig = 1.0 / (1.0 + jnp.exp(-mixed))
        act[r] = (mixed * sig).astype(BF)
        grad = cotangent[r].astype(F32) * sig * (1.0 + mixed * (1.0 - sig))
        low = grad.astype(BF).astype(F32)
        flipped[r] = low.T.astype(BF)
        return total + jnp.sum(low.reshape(side // 8, 8, width), axis=0)

    grad_bias[...] = lax.fori_loop(0, panels, middle, jnp.zeros((8, width), F32))

    def backward(i, carry):
        at = [i * UNROLL + u for u in range(UNROLL)]
        prods = [
            jnp.dot(flipped[row_of(s)], vals[s], preferred_element_type=F32) for s in at
        ]
        for s, prod in zip(at, prods):
            col = jnp.where(s < count, col_of(s), spread)
            grads[col] += prod
        return carry

    lax.fori_loop(0, (count + UNROLL - 1) // UNROLL, backward, 0)

    def store(p, carry):
        partial[p] = grads[p].astype(BF)
        return carry

    lax.fori_loop(0, spread, store, 0)


def reduce_kernel(
    n, shared, partial, nodes, weight, grad_bias,
    grad_feats, grad_weight, bias_out,
    from_twin, from_across, from_z, far, mid, work,
    share, gathered, biases, own_bias,
    send_sem, recv_sem, small_send, small_recv,
):
    me, q, j, y, c, up, down, across, twin = places(n)
    nj = (1 - y) * 2 + c
    tj = y * 2 + (1 - c)
    fj = (1 - y) * 2 + (1 - c)
    panels = partial.shape[1]
    half = panels // PARTS
    direct = PARTS - RELAYED
    if shared:
        greet([(me + d) % n for d in range(1, n)])
    else:
        greet((up, down, across, twin))
    sent = []

    def push(src, dst, key, device):
        k = len(sent)
        copy = send(src, dst, send_sem.at[k], recv_sem.at[key], device)
        sent.append(copy)

    def arrived(dst, key):
        pltpu.make_async_remote_copy(
            src_ref=dst,
            dst_ref=dst,
            send_sem=send_sem.at[0],
            recv_sem=recv_sem.at[key],
            device_id=(lax.axis_index("grp"), twin),
            device_id_type=MESH,
        ).wait_recv()

    def part(ref, index, h):
        return ref.at[index, pl.ds(h * half, half)]

    def merge(dst, a, b):
        def body(p, carry):
            dst[p] = (a[p].astype(F32) + b[p].astype(F32)).astype(BF)
            return carry

        lax.fori_loop(0, half, body, 0)

    order = [
        (0, 2 * y * QUAD + fj),
        (1, QUAD + fj),
        (2, 2 * c * QUAD + tj),
        (3, QUAD + tj),
    ]
    turns = []
    for i in range(PARTS):
        turns += [h for h in (PARTS - 1 - i, i) if h not in turns]
    for k, index in order:
        for h in turns:
            push(part(partial, index, h), part(from_twin, k, h), k * PARTS + h, twin)
    if shared:
        small = []
        own_bias[...] = grad_bias[...]
        for d in range(1, n):
            small.append(
                send(own_bias, biases.at[me], small_send.at[0, d], small_recv.at[0, me],
                     (me + d) % n)
            )
        biases[me] = grad_bias[...]

    back = (1 - y) * down + y * up
    for h in turns:
        arrived(part(from_twin, 0, h), h)
        merge(part(mid, 0, h), part(partial, 2 * y * QUAD + nj, h), part(from_twin, 0, h))
        push(part(mid, 0, h), part(far, 0, h), 4 * PARTS + h, across if h < direct else back)
    near = 2 * (1 - y)
    zs, zo = 2 * (1 - c), 2 * c
    near_at = 1 + (near == zs).astype(jnp.int32)
    zs_up = (zs == 2).astype(jnp.int32)
    to_zs = zs_up * up + (1 - zs_up) * down
    to_zo = (1 - zs_up) * up + zs_up * down

    def beside(h, joined):
        arrived(part(from_twin, 2, h), 2 * PARTS + h)
        merge(part(mid, 2, h), part(partial, zs * QUAD + j, h), part(from_twin, 2, h))

        def fill(p, carry):
            mid[1, h * half + p] = partial[zo * QUAD + j, h * half + p]
            return carry

        lax.fori_loop(0, half, fill, 0)
        if joined:
            arrived(part(far, 0, h), 4 * PARTS + h)
            merge(part(mid, near_at, h), part(mid, near_at, h), part(far, 0, h))
        push(part(mid, 2, h), part(from_z, 1 - zs_up, h), (6 - zs_up) * PARTS + h, to_zs)
        push(part(mid, 1, h), part(from_z, zs_up, h), (5 + zs_up) * PARTS + h, to_zo)

    def over(h, joined):
        arrived(part(from_twin, 1, h), PARTS + h)
        merge(part(mid, 3, h), part(partial, QUAD + nj, h), part(from_twin, 1, h))
        if joined:
            arrived(part(far, 0, h), 4 * PARTS + h)
            merge(part(mid, 3, h), part(mid, 3, h), part(far, 0, h))
        push(part(mid, 3, h), part(from_across, 0, h), 7 * PARTS + h, across)

    for h in turns:
        if h < direct:
            over(h, False)
        else:
            beside(h, False)
    for h in turns:
        if h < direct:
            beside(h, True)
        else:
            over(h, True)

    work[...] = jnp.zeros_like(work)
    for h in turns:
        arrived(part(from_twin, 3, h), 3 * PARTS + h)
        arrived(part(from_z, 0, h), 5 * PARTS + h)
        arrived(part(from_z, 1, h), 6 * PARTS + h)
        arrived(part(from_across, 0, h), 7 * PARTS + h)

        def finish(i, carry, h=h):
            p = h * half + i
            total = partial[QUAD + j, p].astype(F32) + from_twin[3, p].astype(F32)
            total = total + from_across[0, p].astype(F32)
            total = total + from_z[0, p].astype(F32) + from_z[1, p].astype(F32)
            low = total.astype(BF)
            work[...] += jnp.dot(low, nodes[p], preferred_element_type=F32)
            flat = total.T.astype(BF)
            grad_feats[p] = lax.dot_general(
                flat, weight[...], (((1,), (1,)), ((), ())), preferred_element_type=F32
            ).astype(BF)
            return carry

        lax.fori_loop(0, half, finish, 0)

    if shared:
        step = work.shape[0] // n

        def small_wait(dst, level, source):
            pltpu.make_async_remote_copy(
                src_ref=dst,
                dst_ref=dst,
                send_sem=small_send.at[0, 0],
                recv_sem=small_recv.at[level, source],
                device_id=(lax.axis_index("grp"), twin),
                device_id_type=MESH,
            ).wait_recv()

        for d in range(1, n):
            peer = (me + d) % n
            small.append(
                send(work.at[pl.ds(peer * step, step), :], share.at[me],
                     small_send.at[1, d], small_recv.at[1, me], peer)
            )
        share[me] = work[pl.ds(pl.multiple_of(me * step, step), step), :]
        for d in range(1, n):
            small_wait(share.at[(me + d) % n], 1, (me + d) % n)
        gathered[me] = jnp.sum(share[...], axis=0)
        for d in range(1, n):
            small.append(
                send(gathered.at[me], gathered.at[me], small_send.at[2, d],
                     small_recv.at[2, me], (me + d) % n)
            )
        for d in range(1, n):
            small_wait(biases.at[(me + d) % n], 0, (me + d) % n)
        bias_out[...] = jnp.sum(jnp.sum(biases[...], axis=0), axis=0, keepdims=True)
        for d in range(1, n):
            small_wait(gathered.at[(me + d) % n], 2, (me + d) % n)
        grad_weight[...] = gathered[...].reshape(work.shape).T
        for copy in small:
            copy.wait_send()
    else:
        grad_weight[...] = work[...].T
        bias_out[...] = jnp.sum(grad_bias[...], axis=0, keepdims=True)
    for copy in sent:
        copy.wait_send()


def on_device(
    feats, node_order, weight, bias, block_vals, block_rows, block_cols, block_counts, cotangent
):
    row_count, width_in = feats.shape
    slots, side, _ = block_vals.shape
    width = weight.shape[1]
    panels = row_count // side
    n = lax.axis_size("blk")
    pieces = 3 * QUAD

    nodes, projected = pl.pallas_call(
        gather_kernel,
        out_shape=(
            jax.ShapeDtypeStruct((row_count, width_in), BF),
            jax.ShapeDtypeStruct((row_count, width), BF),
        ),
        in_specs=[smem(), vmem(), vmem()],
        out_specs=(vmem(), vmem()),
        scratch_shapes=[
            pltpu.VMEM((row_count, width_in), F32),
            pltpu.VMEM((row_count, width_in), F32),
        ],
        compiler_params=pltpu.CompilerParams(vmem_limit_bytes=VMEM_LIMIT),
        name="gather_project",
    )(node_order, feats, weight)

    window = pl.pallas_call(
        functools.partial(window_kernel, n),
        out_shape=jax.ShapeDtypeStruct((pieces, row_count, width), BF),
        in_specs=[vmem()],
        out_specs=anywhere(),
        scratch_shapes=[
            pltpu.SemaphoreType.DMA((8 * PARTS,)),
            pltpu.SemaphoreType.DMA((pieces, PARTS)),
            pltpu.SemaphoreType.DMA,
        ],
        compiler_params=pltpu.CompilerParams(
            collective_id=0, has_side_effects=True, vmem_limit_bytes=VMEM_LIMIT
        ),
        name="window",
    )(projected)

    spread = pieces * panels
    act, partial, bias_part = pl.pallas_call(
        functools.partial(spmm_kernel, n),
        out_shape=(
            jax.ShapeDtypeStruct((panels, side, width), BF),
            jax.ShapeDtypeStruct((spread, width, side), BF),
            jax.ShapeDtypeStruct((8, width), F32),
        ),
        in_specs=[smem(), smem(), smem(), anywhere(), vmem(), vmem(), anywhere()],
        out_specs=(vmem(), vmem(), vmem()),
        scratch_shapes=[
            pltpu.VMEM((slots, side, side), BF),
            pltpu.VMEM((spread, side, width), BF),
            pltpu.VMEM((panels + 1, side, width), F32),
            pltpu.VMEM((panels, width, side), BF),
            pltpu.VMEM((spread + 1, width, side), F32),
            pltpu.SemaphoreType.DMA((CHUNKS,)),
            pltpu.SemaphoreType.DMA,
        ],
        compiler_params=pltpu.CompilerParams(vmem_limit_bytes=VMEM_LIMIT),
        name="sparse_products",
    )(
        block_counts, block_rows, block_cols,
        window.reshape(spread, side, width), bias.reshape(1, width),
        cotangent.reshape(panels, side, width), block_vals,
    )

    shared = width % (8 * n) == 0
    few = n if shared else 1
    step = width // n if shared else 8
    grad_feats, grad_weight, grad_bias = pl.pallas_call(
        functools.partial(reduce_kernel, n, shared),
        out_shape=(
            jax.ShapeDtypeStruct((panels, side, width_in), BF),
            jax.ShapeDtypeStruct((width_in, width), F32),
            jax.ShapeDtypeStruct((1, width), F32),
        ),
        in_specs=[vmem()] * 4,
        out_specs=(vmem(), vmem(), vmem()),
        scratch_shapes=[
            pltpu.VMEM((4, panels, width, side), BF),
            pltpu.VMEM((1, panels, width, side), BF),
            pltpu.VMEM((2, panels, width, side), BF),
            pltpu.VMEM((1, panels, width, side), BF),
            pltpu.VMEM((4, panels, width, side), BF),
            pltpu.VMEM((width, width_in), F32),
            pltpu.VMEM((few, step, width_in), F32),
            pltpu.VMEM((few, step, width_in), F32),
            pltpu.VMEM((few, 8, width), F32),
            pltpu.VMEM((8, width), F32),
            pltpu.SemaphoreType.DMA((8 * PARTS,)),
            pltpu.SemaphoreType.DMA((8 * PARTS,)),
            pltpu.SemaphoreType.DMA((3, few)),
            pltpu.SemaphoreType.DMA((3, few)),
        ],
        compiler_params=pltpu.CompilerParams(
            collective_id=1, has_side_effects=True, vmem_limit_bytes=VMEM_LIMIT
        ),
        name="reduce_back",
    )(
        partial.reshape(pieces, panels, width, side),
        nodes.reshape(panels, side, width_in), weight, bias_part,
    )
    grad_bias = grad_bias.reshape(width)
    if not shared:
        grad_weight, grad_bias = lax.psum((grad_weight, grad_bias), "blk")
    return (
        act.reshape(row_count, width),
        grad_feats.reshape(row_count, width_in),
        grad_weight,
        grad_bias,
    )


def solution(mesh):
    in_specs = (
        P(("grp", "blk"), None),
        P(("grp", "blk")),
        P(),
        P(),
        P(("grp", "blk"), None, None),
        P(("grp", "blk")),
        P(("grp", "blk")),
        P(("grp", "blk")),
        P(("grp", "blk"), None),
    )
    out_specs = (P(("grp", "blk"), None), P(("grp", "blk"), None), P("grp", None), P("grp"))
    return jax.shard_map(
        on_device, mesh=mesh, in_specs=in_specs, out_specs=out_specs, check_vma=False
    )
```

```python
import functools

import jax
import jax.numpy as jnp
from jax import lax
from jax.experimental import pallas as pl
from jax.experimental.pallas import tpu as pltpu
from jax.sharding import PartitionSpec as P

QUAD = 4
CHUNKS = 7
UNROLL = 24
PARTS = 4
RELAYED = 0
BF = jnp.bfloat16
F32 = jnp.float32
MESH = pl.DeviceIdType.MESH
VMEM_LIMIT = 58 * 1024 * 1024


def vmem():
    return pl.BlockSpec(memory_space=pltpu.VMEM)


def anywhere():
    return pl.BlockSpec(memory_space=pl.ANY)


def smem():
    return pl.BlockSpec(memory_space=pltpu.SMEM)


def gather_kernel(order, feats, weight, nodes, projected, wide, picked):
    count = feats.shape[0]
    first = lax.axis_index("blk") * count
    wide[...] = feats[...].astype(F32)

    def body(i, carry):
        base = pl.multiple_of(i * 32, 32)
        taken = [wide[pl.ds(order[base + u] - first, 1), :] for u in range(32)]
        for u in range(32):
            picked[pl.ds(base + u, 1), :] = taken[u]
        return carry

    lax.fori_loop(0, count // 32, body, 0)
    part = 512 if count % 512 == 0 else count

    def product(i, carry):
        at = pl.ds(pl.multiple_of(i * part, part), part)
        rows = picked[at, :].astype(BF)
        nodes[at, :] = rows
        projected[at, :] = jnp.dot(rows, weight[...], preferred_element_type=F32).astype(BF)
        return carry

    lax.fori_loop(0, count // part, product, 0, unroll=True)


def places(n):
    me = lax.axis_index("blk")
    q, j = me // QUAD, me % QUAD
    y, c = j // 2, j % 2
    quads = n // QUAD
    up = ((q + 1) % quads) * QUAD + j
    down = ((q + quads - 1) % quads) * QUAD + j
    across = q * QUAD + (1 - y) * 2 + c
    twin = q * QUAD + y * 2 + (1 - c)
    return me, q, j, y, c, up, down, across, twin


def greet(devices):
    barrier = pltpu.get_barrier_semaphore()
    for device in devices:
        pl.semaphore_signal(
            barrier, inc=1, device_id=(lax.axis_index("grp"), device), device_id_type=MESH
        )
    pl.semaphore_wait(barrier, len(devices))


def send(src, dst, send_sem, recv_sem, device):
    copy = pltpu.make_async_remote_copy(
        src_ref=src,
        dst_ref=dst,
        send_sem=send_sem,
        recv_sem=recv_sem,
        device_id=(lax.axis_index("grp"), device),
        device_id_type=MESH,
    )
    copy.start()
    return copy


def window_kernel(n, own, window, send_sem, recv_sem, local_sem):
    me, q, j, y, c, up, down, across, twin = places(n)
    nj = (1 - y) * 2 + c
    tj = y * 2 + (1 - c)
    fj = (1 - y) * 2 + (1 - c)
    beyond = (1 - y) * up + y * down
    half = own.shape[0] // PARTS
    greet((up, down, across, twin))
    sent = []

    def piece(slot, p, h):
        return window.at[slot * QUAD + p, pl.ds(h * half, half), :]

    def push(src, slot, p, h, device):
        k = len(sent)
        sent.append(
            send(src, piece(slot, p, h), send_sem.at[k], recv_sem.at[slot * QUAD + p, h], device)
        )

    def arrived(slot, p, h):
        spot = piece(slot, p, h)
        pltpu.make_async_remote_copy(
            src_ref=spot,
            dst_ref=spot,
            send_sem=send_sem.at[0],
            recv_sem=recv_sem.at[slot * QUAD + p, h],
            device_id=(lax.axis_index("grp"), twin),
            device_id_type=MESH,
        ).wait_recv()
        return spot

    def mine(h):
        return own.at[pl.ds(h * half, half), :]

    direct = PARTS - RELAYED
    near, other = 2 * (1 - y), 2 * y
    zs, zo = 2 * (1 - c), 2 * c
    for i in range(PARTS):
        push(mine(PARTS - 1 - i), 1, j, PARTS - 1 - i, across)
        push(mine(i), 0, j, i, up)
        push(mine(i), 2, j, i, down)
    for h in range(PARTS):
        push(mine(h), 1, j, h, twin)
    keep = pltpu.make_async_copy(own, window.at[QUAD + j], local_sem)
    keep.start()
    for i in range(PARTS):
        h = PARTS - 1 - i
        spot = arrived(1, nj, h)
        if h >= direct:
            push(spot, 2 * y, nj, h, beyond)
        push(spot, 1, nj, h, twin)
        spot = arrived(near, j, i)
        if i < direct:
            push(spot, near, j, i, across)
        arrived(other, j, i)
        push(piece(zs, j, i), zs, j, i, twin)
    far = []
    for i in range(PARTS):
        far += [h for h in (PARTS - 1 - i, i) if h not in far]
    for h in far:
        push(arrived(2 * y, nj, h), 2 * y, nj, h, twin)
    for h in range(PARTS):
        arrived(1, tj, h)
        arrived(1, fj, h)
        arrived(zo, tj, h)
        arrived(2 * y, fj, h)
    keep.wait()
    for copy in sent:
        copy.wait_send()


def spmm_kernel(
    n, counts, block_rows, block_cols, window_hbm, bias, cotangent, vals_hbm,
    act, partial, grad_bias, vals, window, acc, flipped, grads, sems, window_sem,
):
    slots, side, width = vals_hbm.shape
    panels = acc.shape[0] - 1
    spread = grads.shape[0] - 1
    per = slots // CHUNKS
    count = counts[0]
    me = lax.axis_index("blk")
    quads = n // QUAD
    first_row = me * panels
    first_col = lax.rem(me // QUAD + quads - 1, quads) * (QUAD * panels)
    fill = pltpu.make_async_copy(window_hbm, window, window_sem)
    fill.start()

    def row_of(s):
        return block_rows[s] - first_row

    def col_of(s):
        away = block_cols[s] - first_col
        return jnp.where(away < 0, away + n * panels, away)

    def fetch(k):
        at = pl.ds(k * per, per)
        return pltpu.make_async_copy(vals_hbm.at[at], vals.at[at], sems.at[k])

    for k in range(CHUNKS):
        @pl.when(k * per < count)
        def _(k=k):
            fetch(k).start()

    acc[...] = jnp.zeros_like(acc)

    def clear(p, carry):
        grads[p] = jnp.zeros((side, width), F32)
        return carry

    lax.fori_loop(0, spread, clear, 0, unroll=4)
    fill.wait()

    def forward(i, carry):
        at = [i * UNROLL + u for u in range(UNROLL)]
        prods = [
            jnp.dot(vals[s], window[col_of(s)], preferred_element_type=F32) for s in at
        ]
        for s, prod in zip(at, prods):
            row = jnp.where(s < count, row_of(s), panels)
            acc[row] += prod
        return carry

    for k in range(CHUNKS):
        @pl.when(k * per < count)
        def _(k=k):
            fetch(k).wait()
            lax.fori_loop(k * per // UNROLL, (k + 1) * per // UNROLL, forward, 0)

    def middle(r, total):
        mixed = acc[r] + bias[...]
        sig = 1.0 / (1.0 + jnp.exp(-mixed))
        act[r] = (mixed * sig).astype(BF)
        grad = cotangent[r].astype(F32) * sig * (1.0 + mixed * (1.0 - sig))
        low = grad.astype(BF).astype(F32)
        flipped[r] = low.T.astype(BF)
        return total + jnp.sum(low.reshape(side // 8, 8, width), axis=0)

    grad_bias[...] = lax.fori_loop(0, panels, middle, jnp.zeros((8, width), F32), unroll=4)

    def backward(i, carry):
        at = [i * UNROLL + u for u in range(UNROLL)]
        prods = [
            jnp.dot(flipped[row_of(s)], vals[s], preferred_element_type=F32) for s in at
        ]
        for s, prod in zip(at, prods):
            col = jnp.where(s < count, col_of(s), spread)
            grads[col] += prod
        return carry

    lax.fori_loop(0, (count + UNROLL - 1) // UNROLL, backward, 0)

    def store(p, carry):
        partial[p] = grads[p].astype(BF)
        return carry

    lax.fori_loop(0, spread, store, 0, unroll=4)


def reduce_kernel(
    n, shared, partial, nodes, weight, grad_bias,
    grad_feats, grad_weight, bias_out,
    from_twin, from_across, from_z, far, mid, work,
    share, gathered, biases, own_bias,
    send_sem, recv_sem, small_send, small_recv,
):
    me, q, j, y, c, up, down, across, twin = places(n)
    nj = (1 - y) * 2 + c
    tj = y * 2 + (1 - c)
    fj = (1 - y) * 2 + (1 - c)
    panels = partial.shape[1]
    half = panels // PARTS
    direct = PARTS - RELAYED
    if shared:
        greet([(me + d) % n for d in range(1, n)])
    else:
        greet((up, down, across, twin))
    sent = []

    def push(src, dst, key, device):
        k = len(sent)
        copy = send(src, dst, send_sem.at[k], recv_sem.at[key], device)
        sent.append(copy)

    def arrived(dst, key):
        pltpu.make_async_remote_copy(
            src_ref=dst,
            dst_ref=dst,
            send_sem=send_sem.at[0],
            recv_sem=recv_sem.at[key],
            device_id=(lax.axis_index("grp"), twin),
            device_id_type=MESH,
        ).wait_recv()

    def part(ref, index, h):
        return ref.at[index, pl.ds(h * half, half)]

    def merge(dst, a, b):
        def body(p, carry):
            dst[p] = (a[p].astype(F32) + b[p].astype(F32)).astype(BF)
            return carry

        lax.fori_loop(0, half, body, 0, unroll=True)

    order = [
        (0, 2 * y * QUAD + fj),
        (1, QUAD + fj),
        (2, 2 * c * QUAD + tj),
        (3, QUAD + tj),
    ]
    turns = []
    for i in range(PARTS):
        turns += [h for h in (PARTS - 1 - i, i) if h not in turns]
    for k, index in order:
        for h in turns:
            push(part(partial, index, h), part(from_twin, k, h), k * PARTS + h, twin)
    if shared:
        small = []
        own_bias[...] = grad_bias[...]
        for d in range(1, n):
            small.append(
                send(own_bias, biases.at[me], small_send.at[0, d], small_recv.at[0, me],
                     (me + d) % n)
            )
        biases[me] = grad_bias[...]

    back = (1 - y) * down + y * up
    for h in turns:
        arrived(part(from_twin, 0, h), h)
        merge(part(mid, 0, h), part(partial, 2 * y * QUAD + nj, h), part(from_twin, 0, h))
        push(part(mid, 0, h), part(far, 0, h), 4 * PARTS + h, across if h < direct else back)
    near = 2 * (1 - y)
    zs, zo = 2 * (1 - c), 2 * c
    near_at = 1 + (near == zs).astype(jnp.int32)
    zs_up = (zs == 2).astype(jnp.int32)
    to_zs = zs_up * up + (1 - zs_up) * down
    to_zo = (1 - zs_up) * up + zs_up * down

    def beside(h, joined):
        arrived(part(from_twin, 2, h), 2 * PARTS + h)
        merge(part(mid, 2, h), part(partial, zs * QUAD + j, h), part(from_twin, 2, h))

        def fill(p, carry):
            mid[1, h * half + p] = partial[zo * QUAD + j, h * half + p]
            return carry

        lax.fori_loop(0, half, fill, 0, unroll=True)
        if joined:
            arrived(part(far, 0, h), 4 * PARTS + h)
            merge(part(mid, near_at, h), part(mid, near_at, h), part(far, 0, h))
        push(part(mid, 2, h), part(from_z, 1 - zs_up, h), (6 - zs_up) * PARTS + h, to_zs)
        push(part(mid, 1, h), part(from_z, zs_up, h), (5 + zs_up) * PARTS + h, to_zo)

    def over(h, joined):
        arrived(part(from_twin, 1, h), PARTS + h)
        merge(part(mid, 3, h), part(partial, QUAD + nj, h), part(from_twin, 1, h))
        if joined:
            arrived(part(far, 0, h), 4 * PARTS + h)
            merge(part(mid, 3, h), part(mid, 3, h), part(far, 0, h))
        push(part(mid, 3, h), part(from_across, 0, h), 7 * PARTS + h, across)

    for h in turns:
        if h < direct:
            over(h, False)
        else:
            beside(h, False)
    for h in turns:
        if h < direct:
            beside(h, True)
        else:
            over(h, True)

    work[...] = jnp.zeros_like(work)
    for h in turns:
        arrived(part(from_twin, 3, h), 3 * PARTS + h)
        arrived(part(from_z, 0, h), 5 * PARTS + h)
        arrived(part(from_z, 1, h), 6 * PARTS + h)
        arrived(part(from_across, 0, h), 7 * PARTS + h)

        def finish(i, carry, h=h):
            p = h * half + i
            total = partial[QUAD + j, p].astype(F32) + from_twin[3, p].astype(F32)
            total = total + from_across[0, p].astype(F32)
            total = total + from_z[0, p].astype(F32) + from_z[1, p].astype(F32)
            low = total.astype(BF)
            work[...] += jnp.dot(low, nodes[p], preferred_element_type=F32)
            flat = total.T.astype(BF)
            grad_feats[p] = lax.dot_general(
                flat, weight[...], (((1,), (1,)), ((), ())), preferred_element_type=F32
            ).astype(BF)
            return carry

        lax.fori_loop(0, half, finish, 0, unroll=True)

    if shared:
        step = work.shape[0] // n

        def small_wait(dst, level, source):
            pltpu.make_async_remote_copy(
                src_ref=dst,
                dst_ref=dst,
                send_sem=small_send.at[0, 0],
                recv_sem=small_recv.at[level, source],
                device_id=(lax.axis_index("grp"), twin),
                device_id_type=MESH,
            ).wait_recv()

        for d in range(1, n):
            peer = (me + d) % n
            small.append(
                send(work.at[pl.ds(peer * step, step), :], share.at[me],
                     small_send.at[1, d], small_recv.at[1, me], peer)
            )
        share[me] = work[pl.ds(pl.multiple_of(me * step, step), step), :]
        for d in range(1, n):
            small_wait(share.at[(me + d) % n], 1, (me + d) % n)
        gathered[me] = jnp.sum(share[...], axis=0)
        for d in range(1, n):
            small.append(
                send(gathered.at[me], gathered.at[me], small_send.at[2, d],
                     small_recv.at[2, me], (me + d) % n)
            )
        for d in range(1, n):
            small_wait(biases.at[(me + d) % n], 0, (me + d) % n)
        bias_out[...] = jnp.sum(jnp.sum(biases[...], axis=0), axis=0, keepdims=True)
        for d in range(1, n):
            small_wait(gathered.at[(me + d) % n], 2, (me + d) % n)
        grad_weight[...] = gathered[...].reshape(work.shape).T
        for copy in small:
            copy.wait_send()
    else:
        grad_weight[...] = work[...].T
        bias_out[...] = jnp.sum(grad_bias[...], axis=0, keepdims=True)
    for copy in sent:
        copy.wait_send()


def on_device(
    feats, node_order, weight, bias, block_vals, block_rows, block_cols, block_counts, cotangent
):
    row_count, width_in = feats.shape
    slots, side, _ = block_vals.shape
    width = weight.shape[1]
    panels = row_count // side
    n = lax.axis_size("blk")
    pieces = 3 * QUAD

    nodes, projected = pl.pallas_call(
        gather_kernel,
        out_shape=(
            jax.ShapeDtypeStruct((row_count, width_in), BF),
            jax.ShapeDtypeStruct((row_count, width), BF),
        ),
        in_specs=[smem(), vmem(), vmem()],
        out_specs=(vmem(), vmem()),
        scratch_shapes=[
            pltpu.VMEM((row_count, width_in), F32),
            pltpu.VMEM((row_count, width_in), F32),
        ],
        compiler_params=pltpu.CompilerParams(vmem_limit_bytes=VMEM_LIMIT),
        name="gather_project",
    )(node_order, feats, weight)

    window = pl.pallas_call(
        functools.partial(window_kernel, n),
        out_shape=jax.ShapeDtypeStruct((pieces, row_count, width), BF),
        in_specs=[vmem()],
        out_specs=anywhere(),
        scratch_shapes=[
            pltpu.SemaphoreType.DMA((8 * PARTS,)),
            pltpu.SemaphoreType.DMA((pieces, PARTS)),
            pltpu.SemaphoreType.DMA,
        ],
        compiler_params=pltpu.CompilerParams(
            collective_id=0, has_side_effects=True, vmem_limit_bytes=VMEM_LIMIT
        ),
        name="window",
    )(projected)

    spread = pieces * panels
    act, partial, bias_part = pl.pallas_call(
        functools.partial(spmm_kernel, n),
        out_shape=(
            jax.ShapeDtypeStruct((panels, side, width), BF),
            jax.ShapeDtypeStruct((spread, width, side), BF),
            jax.ShapeDtypeStruct((8, width), F32),
        ),
        in_specs=[smem(), smem(), smem(), anywhere(), vmem(), vmem(), anywhere()],
        out_specs=(vmem(), vmem(), vmem()),
        scratch_shapes=[
            pltpu.VMEM((slots, side, side), BF),
            pltpu.VMEM((spread, side, width), BF),
            pltpu.VMEM((panels + 1, side, width), F32),
            pltpu.VMEM((panels, width, side), BF),
            pltpu.VMEM((spread + 1, width, side), F32),
            pltpu.SemaphoreType.DMA((CHUNKS,)),
            pltpu.SemaphoreType.DMA,
        ],
        compiler_params=pltpu.CompilerParams(vmem_limit_bytes=VMEM_LIMIT),
        name="sparse_products",
    )(
        block_counts, block_rows, block_cols,
        window.reshape(spread, side, width), bias.reshape(1, width),
        cotangent.reshape(panels, side, width), block_vals,
    )

    shared = width % (8 * n) == 0
    few = n if shared else 1
    step = width // n if shared else 8
    grad_feats, grad_weight, grad_bias = pl.pallas_call(
        functools.partial(reduce_kernel, n, shared),
        out_shape=(
            jax.ShapeDtypeStruct((panels, side, width_in), BF),
            jax.ShapeDtypeStruct((width_in, width), F32),
            jax.ShapeDtypeStruct((1, width), F32),
        ),
        in_specs=[vmem()] * 4,
        out_specs=(vmem(), vmem(), vmem()),
        scratch_shapes=[
            pltpu.VMEM((4, panels, width, side), BF),
            pltpu.VMEM((1, panels, width, side), BF),
            pltpu.VMEM((2, panels, width, side), BF),
            pltpu.VMEM((1, panels, width, side), BF),
            pltpu.VMEM((4, panels, width, side), BF),
            pltpu.VMEM((width, width_in), F32),
            pltpu.VMEM((few, step, width_in), F32),
            pltpu.VMEM((few, step, width_in), F32),
            pltpu.VMEM((few, 8, width), F32),
            pltpu.VMEM((8, width), F32),
            pltpu.SemaphoreType.DMA((8 * PARTS,)),
            pltpu.SemaphoreType.DMA((8 * PARTS,)),
            pltpu.SemaphoreType.DMA((3, few)),
            pltpu.SemaphoreType.DMA((3, few)),
        ],
        compiler_params=pltpu.CompilerParams(
            collective_id=1, has_side_effects=True, vmem_limit_bytes=VMEM_LIMIT
        ),
        name="reduce_back",
    )(
        partial.reshape(pieces, panels, width, side),
        nodes.reshape(panels, side, width_in), weight, bias_part,
    )
    grad_bias = grad_bias.reshape(width)
    if not shared:
        grad_weight, grad_bias = lax.psum((grad_weight, grad_bias), "blk")
    return (
        act.reshape(row_count, width),
        grad_feats.reshape(row_count, width_in),
        grad_weight,
        grad_bias,
    )


def solution(mesh):
    in_specs = (
        P(("grp", "blk"), None),
        P(("grp", "blk")),
        P(),
        P(),
        P(("grp", "blk"), None, None),
        P(("grp", "blk")),
        P(("grp", "blk")),
        P(("grp", "blk")),
        P(("grp", "blk"), None),
    )
    out_specs = (P(("grp", "blk"), None), P(("grp", "blk"), None), P("grp", None), P("grp"))
    return jax.shard_map(
        on_device, mesh=mesh, in_specs=in_specs, out_specs=out_specs, check_vma=False
    )
```
